32 devices in a mesh: groups: 2 (over y), tensor: 16 (over z, x, core).
Axes of the slice: x: 2, y: 2, z: 4, core: 2. Of those that a mesh axis runs over, the one named last changes fastest.
Arguments:
- tokens: bfloat16 [64, 8192], P(('groups', 'tensor')), parts along dimension 0, may hold values from -6 to 6
- norm_gain: float32 [8192], replicated, may hold values from 0.1 to 1.9
- token_order: int32 [64], P('groups'), parts along dimension 0, may hold values from 0 to 31, each once
- gate_weight: bfloat16 [8192, 16384], P(None, 'tensor'), may hold values from -0.09375 to 0.09375
- gate_keep: int32 [128, 256], P(None, 'tensor'), may hold values 0 or 1
- gate_expo: int32 [128, 256], P(None, 'tensor'), may hold values from -1 to 1
- up_weight: bfloat16 [8192, 16384], P(None, 'tensor'), may hold values from -0.09375 to 0.09375
- up_keep: int32 [128, 256], P(None, 'tensor'), may hold values 0 or 1
- up_expo: int32 [128, 256], P(None, 'tensor'), may hold values from -1 to 1
- down_weight: bfloat16 [16384, 8192], P('tensor'), may hold values from -0.0625 to 0.0625
- down_keep: int32 [256, 128], P('tensor'), may hold values 0 or 1
- down_expo: int32 [256, 128], P('tensor'), may hold values from -1 to 1
Outputs:
- ffn_out: bfloat16 [64, 8192], P(('groups', 'tensor')), parts along dimension 0
The draws below stay inside these ranges and needn't reach their ends.
There are 2 independent parts, one for each index of `groups`. The reference program is written for one: setup_inputs(seed, part) draws one part's arguments, and reference() takes and returns one part's arrays. A program takes and returns all parts, laid end to end along the dimension named above; an argument that names none is the same for every part. Nothing has to cross between parts.
Inputs may be any that keep to these rules, and one draw needn't show every extreme that they name: `token_order`: each token appears exactly once.
All inputs are finite; a program needn't handle non-finite values. No bound on the sum of `gate_keep` or of `up_keep` or of `down_keep` on one device may be relied on, other than what follows from the above.
Results may differ from the reference program's by a relative error of at most 0.0065.
Values may be sent and summed in bfloat16 or wider, within the bound.
A program may use at most 128 MiB of HBM per device.

```python
import jax
import jax.numpy as jnp
from jax import lax

D = 8192
FF = 16384
BLOCK = 64
TOKENS = 32


def set_ends(drawn, rng, low, high):
    longest = drawn.shape.index(max(drawn.shape))
    spots = []
    for shift in (0, 1):
        where = [jax.random.randint(jax.random.fold_in(rng, axis), (), 0, length) for axis, length in enumerate(drawn.shape)]
        where[longest] = (where[longest] + shift) % drawn.shape[longest]
        spots.append(tuple(where))
    return drawn.at[spots[0]].set(low).at[spots[1]].set(high)


def block_scale(key, shape, pieces, low, top_value):
    def one(dim, parts):
        draws = jax.random.uniform(jax.random.fold_in(jax.random.fold_in(key, 6), dim), (parts,), jnp.float32, low / len(pieces), top_value / len(pieces))
        return jnp.repeat(jnp.exp(draws), shape[dim] // parts).reshape((-1,) + (1,) * (len(shape) - dim - 1))

    gain = one(*pieces[0])
    for cut in pieces[1:]:
        gain = gain * one(*cut)
    return gain


def centred(rng, extent, scale, reach, shards=(), dtype=jnp.bfloat16):
    loudness = block_scale(rng, extent, shards, -0.22, 0.18) if shards else 1.0
    entries = jax.random.normal(rng, extent, jnp.float32) * scale * loudness
    return jnp.minimum(jnp.maximum(entries, -reach), reach).astype(dtype)


def setup_inputs(seed: int = 0, part: int = 0) -> dict:
    splits = jax.random.split(jax.random.key(seed), 13)
    own_keys = jax.random.split(jax.random.fold_in(splits[12], part), 13)
    tokens = centred(own_keys[0], (TOKENS, D), 1.0, 6.0, ((0, 16),))
    norm_gain = jnp.clip(1.0 + 0.18 * jax.random.normal(splits[1], (D,), jnp.float32), 0.1, 1.9)
    token_order = jax.random.permutation(own_keys[2], TOKENS).astype(jnp.int32)
    gate_weight = centred(splits[3], (D, FF), (D // 2) ** -0.5, 0.09375, ((1, 16),))
    gate_keep = set_ends((jax.random.randint(splits[4], (D // BLOCK, FF // BLOCK), 0, 2) < 1).astype(jnp.int32), jax.random.fold_in(splits[4], 1), 0, 1)
    gate_expo = set_ends(jax.random.randint(splits[5], (D // BLOCK, FF // BLOCK), -1, 2), jax.random.fold_in(splits[5], 1), -1, 1).astype(jnp.int32)
    up_weight = centred(splits[6], (D, FF), (D // 2) ** -0.5, 0.09375, ((1, 16),))
    up_keep = set_ends((jax.random.randint(splits[7], (D // BLOCK, FF // BLOCK), 0, 2) < 1).astype(jnp.int32), jax.random.fold_in(splits[7], 1), 0, 1)
    up_expo = set_ends(jax.random.randint(splits[8], (D // BLOCK, FF // BLOCK), -1, 2), jax.random.fold_in(splits[8], 1), -1, 1).astype(jnp.int32)
    down_weight = centred(splits[9], (FF, D), (FF // 2) ** -0.5, 0.0625, ((0, 16),))
    down_keep = set_ends((jax.random.randint(splits[10], (FF // BLOCK, D // BLOCK), 0, 2) < 1).astype(jnp.int32), jax.random.fold_in(splits[10], 1), 0, 1)
    down_expo = set_ends(jax.random.randint(splits[11], (FF // BLOCK, D // BLOCK), -1, 2), jax.random.fold_in(splits[11], 1), -1, 1).astype(jnp.int32)
    return {"tokens": tokens, "norm_gain": norm_gain, "token_order": token_order, "gate_weight": gate_weight, "gate_keep": gate_keep, "gate_expo": gate_expo, "up_weight": up_weight, "up_keep": up_keep, "up_expo": up_expo, "down_weight": down_weight, "down_keep": down_keep, "down_expo": down_expo}


def scaled(weight, keep, expo):
    rows, cols = weight.shape
    brow, bcol = keep.shape
    factor = jnp.where(keep > 0, jnp.exp2(expo.astype(jnp.float32)), 0.0).astype(jnp.bfloat16)
    widened = jnp.repeat(factor, cols // bcol, axis=1)
    blocks = weight.reshape(brow, rows // brow, cols) * widened[:, None, :]
    return blocks.reshape(rows, cols)

def normalize(tokens, norm_gain):
    values = tokens.astype(jnp.float32)
    meansq = lax.optimization_barrier(jnp.mean(values * values, axis=-1, keepdims=True))
    return (values * jax.lax.rsqrt(meansq + 1e-05) * norm_gain).astype(jnp.bfloat16)

def reference(tokens, norm_gain, token_order, gate_weight, gate_keep, gate_expo, up_weight, up_keep, up_expo, down_weight, down_keep, down_expo):
    normed = normalize(tokens, norm_gain)
    gate = jnp.dot(normed, scaled(gate_weight, gate_keep, gate_expo), preferred_element_type=jnp.float32)
    up = jnp.dot(normed, scaled(up_weight, up_keep, up_expo), preferred_element_type=jnp.float32)
    hidden = (jax.nn.silu(gate) * up).astype(jnp.bfloat16)
    picked = hidden[token_order.astype(jnp.int32)]
    result = jnp.dot(picked, scaled(down_weight, down_keep, down_expo), preferred_element_type=jnp.float32)
    return result.astype(jnp.bfloat16)
```

```python
import functools

import jax
import jax.numpy as jnp
from jax import lax
from jax.experimental import pallas as pl
from jax.experimental.pallas import tpu as pltpu
from jax.sharding import PartitionSpec as P

BF = jnp.bfloat16
F32 = jnp.float32
CORES = 2
QG = 4
QR = 4
TILE = 16


def grid_of(n):
    chips = n // CORES
    x = 1
    while (2 * x) * (2 * x) < chips:
        x *= 2
    return chips // x, x


def log2(v):
    return v.bit_length() - 1


def iota(shape, dim):
    return lax.broadcasted_iota(jnp.int32, shape, dim)


def factor(keep, expo):
    power = jnp.where(expo == 0, 1.0, jnp.where(expo > 0, 2.0, 0.5))
    return jnp.where(keep > 0, power, 0.0).astype(F32).astype(BF)


def scale_rows(w, fac, side):
    n = w.shape[0] // side
    cols = w.shape[1]
    parts = []
    for j in range(n):
        row = jnp.broadcast_to(fac[j : j + 1, :], (TILE, cols)).astype(BF)
        block = w[j * side : (j + 1) * side, :].reshape(side // TILE, TILE, cols)
        parts.append((block * row[None]).reshape(side, cols))
    return parts[0] if n == 1 else jnp.concatenate(parts, axis=0)


def kernel(
    Z, X,
    tok_h, gain_h, order_h, gw_h, gk_h, ge_h, uw_h, uk_h, ue_h, dw_h, dk_h, de_h,
    out_ref,
    tok, gain, order, gw, gk, ge, uw, uk, ue, dw, dk, de,
    gfac, ufac, dfac, gbuf, lhs, accg, accu, hid,
    part, csend, crecv, ybuf, xsend, xrecv, zbuf, zrecv,
    small_sem, g_sem, u_sem, d_sem,
    gz_s, gz_r, gx_s, gx_r, gc_s, gc_r,
    rc_s, rc_r, rx_s, rx_r, rz_s, rz_r,
):
    C = CORES
    R, D = tok.shape
    F = gw.shape[1]
    T = C * X * Z * R
    G = TILE // R
    side = D // gk.shape[1]
    KCH = D // QG
    PL = KCH // G
    NC = D // QR
    NCG = NC // G

    me = lax.axis_index("tensor")
    mc = lax.rem(me, C)
    mx = lax.rem(lax.div(me, C), X)
    mz = lax.div(me, C * X)

    def dev(z, x, c):
        return {"tensor": (z * X + x) * C + c}

    def zpeer(d):
        return dev(lax.rem(mz + d, Z), mx, mc)

    def xpeer(d):
        return dev(mz, lax.rem(mx + d, X), mc)

    cpeer = dev(mz, mx, 1 - mc)
    MESH = pl.DeviceIdType.MESH

    barrier = pltpu.get_barrier_semaphore()
    for d in range(1, Z):
        pl.semaphore_signal(barrier, inc=1, device_id=zpeer(d), device_id_type=MESH)
    for d in range(1, X):
        pl.semaphore_signal(barrier, inc=1, device_id=xpeer(d), device_id_type=MESH)
    pl.semaphore_signal(barrier, inc=1, device_id=cpeer, device_id_type=MESH)

    smalls = []
    for i, (a, b) in enumerate(
        ((tok_h, tok), (gain_h, gain), (order_h, order), (gk_h, gk), (ge_h, ge),
         (uk_h, uk), (ue_h, ue), (dk_h, dk), (de_h, de))
    ):
        cp = pltpu.make_async_copy(a, b, small_sem.at[i])
        cp.start()
        smalls.append(cp)
    gcp, ucp, dcp = [], [], []
    for q in range(QG):
        rows = pl.ds(q * KCH, KCH)
        gcp.append(pltpu.make_async_copy(gw_h.at[rows], gw.at[rows], g_sem.at[q]))
        ucp.append(pltpu.make_async_copy(uw_h.at[rows], uw.at[rows], u_sem.at[q]))
        gcp[-1].start()
        ucp[-1].start()
    for q in range(QR):
        cols = pl.ds(q * NC, NC)
        dcp.append(pltpu.make_async_copy(dw_h.at[:, cols], dw.at[:, cols], d_sem.at[q]))
        dcp[-1].start()

    smalls[0].wait()
    smalls[1].wait()
    values = tok[...].astype(F32)
    meansq = jnp.sum(values * values, axis=-1, keepdims=True) * (1.0 / D)
    normed = values * lax.rsqrt(meansq + 1e-05) * gain[...]
    for q in range(QG):
        rowid = iota((TILE, PL), 0)
        piece = jnp.zeros((TILE, PL), F32)
        for g in range(G):
            for i in range(R):
                lo = q * KCH + g * PL
                src = jnp.broadcast_to(normed[i : i + 1, lo : lo + PL], (TILE, PL))
                piece = jnp.where(rowid == g * R + i, src, piece)
        gbuf[q, mc, mx, mz] = piece.astype(BF)

    pl.semaphore_wait(barrier, Z + X - 1)

    def remote(src, dst, s, r, to):
        return pltpu.make_async_remote_copy(
            src_ref=src, dst_ref=dst, send_sem=s, recv_sem=r, device_id=to, device_id_type=MESH
        )

    gz, gx, gc = {}, {}, {}
    for q in range(QG):
        for d in range(1, Z):
            ref = gbuf.at[q, mc, mx, mz]
            gz[q, d] = remote(ref, ref, gz_s.at[q, d - 1], gz_r.at[q, d - 1], zpeer(d))
            gz[q, d].start()

    for s in smalls[2:]:
        s.wait()
    spread = (iota((F // side, F), 1) >> log2(side)) == iota((F // side, F), 0)
    spread = spread.astype(F32).astype(BF)
    outer = (((0,), (0,)), ((), ()))
    gfac[...] = lax.dot_general(factor(gk[...], ge[...]), spread, outer, preferred_element_type=F32)
    ufac[...] = lax.dot_general(factor(uk[...], ue[...]), spread, outer, preferred_element_type=F32)

    def gather_x(q):
        for d in range(1, Z):
            gz[q, d].wait_recv()
        for d in range(1, X):
            ref = gbuf.at[q, mc, mx]
            gx[q, d] = remote(ref, ref, gx_s.at[q, d - 1], gx_r.at[q, d - 1], xpeer(d))
            gx[q, d].start()

    def gather_c(q):
        for d in range(1, X):
            gx[q, d].wait_recv()
        ref = gbuf.at[q, mc]
        gc[q] = remote(ref, ref, gc_s.at[q], gc_r.at[q], cpeer)
        gc[q].start()

    for step in range(QG + 1):
        if step < QG:
            gather_x(step)
        if step >= 1:
            gather_c(step - 1)

    dk_fac = factor(dk[...], de[...])
    for q in range(QR):
        wide = (D // side, NC)
        sel = ((iota(wide, 1) + q * NC) >> log2(side)) == iota(wide, 0)
        dfac[:, q * NC : (q + 1) * NC] = jnp.dot(dk_fac, sel.astype(F32).astype(BF), preferred_element_type=F32)

    def token_of(r):
        i = r & (R - 1)
        z = (r >> log2(R)) & (Z - 1)
        x = (r >> log2(R * Z)) & (X - 1)
        c = r >> log2(R * Z * X)
        return ((z * X + x) * C + c) * R + i

    ones = lambda m: m.astype(F32).astype(BF)
    tt = (T, T)
    s_in = ones(token_of(iota(tt, 0)) == iota(tt, 1))
    s_out = ones(token_of(iota(tt, 1)) == iota(tt, 0))
    mt = ones(iota(tt, 0) == jnp.broadcast_to(order[...], tt))
    pt = jnp.dot(s_in, mt, preferred_element_type=F32).astype(BF)
    pt = jnp.dot(pt, s_out, preferred_element_type=F32)
    pick = pt.T.astype(BF)

    nd = TILE * TILE
    o, s = iota((nd, nd), 0), iota((nd, nd), 1)
    og, od, oi = o >> log2(TILE * R), (o >> log2(R)) & (TILE - 1), o & (R - 1)
    perm = ones(s == od * TILE + og * R + oi)

    KS = 8 * side
    for q in range(QG):
        gc[q].wait_recv()
        rows = gbuf[q].reshape(C * X * Z * TILE, PL)
        for b in range(C * X * Z // TILE):
            y = jnp.dot(perm, rows[b * nd : (b + 1) * nd], preferred_element_type=F32).astype(BF)
            n = TILE * R
            for g in range(G):
                lhs[q, b * n : (b + 1) * n, g * PL : (g + 1) * PL] = y[g * n : (g + 1) * n]
        gcp[q].wait()
        ucp[q].wait()
        if q == 0:
            accg[...] = jnp.zeros_like(accg)
            accu[...] = jnp.zeros_like(accu)

        def gate_up(s, carry, q=q):
            ks = pl.ds(pl.multiple_of(q * KCH + s * KS, KS), KS)
            fs = pl.ds(pl.multiple_of((q * KCH + s * KS) // side, 8), 8)
            left = lhs[q, :, pl.ds(pl.multiple_of(s * KS, KS), KS)]
            wg = scale_rows(gw[ks, :], gfac[fs, :], side)
            accg[...] += jnp.dot(left, wg, preferred_element_type=F32)
            wu = scale_rows(uw[ks, :], ufac[fs, :], side)
            accu[...] += jnp.dot(left, wu, preferred_element_type=F32)
            return carry

        lax.fori_loop(0, KCH // KS, gate_up, 0)

    gate = accg[...]
    hidden = (gate / (1.0 + jnp.exp(-gate)) * accu[...]).astype(BF)
    hid[...] = jnp.dot(pick, hidden, preferred_element_type=F32).astype(BF)

    half = X * Z * R
    fold = max(1, TILE // (Z * R))
    zr = Z * R
    zn = G * zr
    o, s = iota((zn, zn), 0), iota((zn, zn), 1)
    oz, og, oi = o >> log2(TILE), (o >> log2(R)) & (G - 1), o & (R - 1)
    perm_z = ones(s == og * zr + oz * R + oi)

    rc, rx, rz = {}, {}, {}

    def folded(v):
        w = NC // fold
        return jnp.concatenate([v[:, h * w : (h + 1) * w] for h in range(fold)], axis=0) if fold > 1 else v

    NS = 512

    def down(q):
        dcp[q].wait()

        def tile(n, carry):
            cols = pl.ds(pl.multiple_of(q * NC + n * NS, NS), NS)
            w = scale_rows(dw[:, cols], dfac[:, cols], side)
            y = jnp.dot(hid[...], w, preferred_element_type=F32)
            part[q, :, :, pl.ds(pl.multiple_of(n * NS, NS), NS)] = y.reshape(C, half, NS)
            return carry

        lax.fori_loop(0, NC // NS, tile, 0)
        csend[q] = part[q, 1 - mc].astype(BF)
        rc[q] = remote(csend.at[q], crecv.at[q], rc_s.at[q], rc_r.at[q], cpeer)
        rc[q].start()

    def reduce_x(q):
        rc[q].wait_recv()
        ybuf[q] = (part[q, mc] + crecv[q].astype(F32)).reshape(X, zr, NC)
        for d in range(1, X):
            xsend[q, d - 1] = folded(ybuf[q, lax.rem(mx + d, X)]).astype(BF)
            rx[q, d] = remote(
                xsend.at[q, d - 1], xrecv.at[q, d - 1], rx_s.at[q, d - 1], rx_r.at[q, d - 1], xpeer(d)
            )
            rx[q, d].start()

    def reduce_z(q):
        y = folded(ybuf[q, mx])
        for d in range(1, X):
            rx[q, d].wait_recv()
            y = y + xrecv[q, d - 1].astype(F32)
        per = G // fold
        stack = [
            y[(g // per) * zr : (g // per + 1) * zr, (g % per) * NCG : (g % per + 1) * NCG] for g in range(G)
        ]
        stack = jnp.concatenate(stack, axis=0).astype(BF)
        zbuf[q] = jnp.dot(perm_z, stack, preferred_element_type=F32).astype(BF).reshape(Z, TILE, NCG)
        for d in range(1, Z):
            rz[q, d] = remote(
                zbuf.at[q, lax.rem(mz + d, Z)], zrecv.at[q, d - 1],
                rz_s.at[q, d - 1], rz_r.at[q, d - 1], zpeer(d),
            )
            rz[q, d].start()

    def finish(q):
        y = zbuf[q, mz].astype(F32)
        for d in range(1, Z):
            rz[q, d].wait_recv()
            y = y + zrecv[q, d - 1].astype(F32)
        for g in range(G):
            for i in range(R):
                lo = q * NC + g * NCG
                out_ref[i : i + 1, lo : lo + NCG] = y[g * R + i : g * R + i + 1]

    for step in range(QR + 3):
        if step < QR:
            down(step)
        if 0 <= step - 1 < QR:
            reduce_x(step - 1)
        if 0 <= step - 2 < QR:
            reduce_z(step - 2)
        if 0 <= step - 3 < QR:
            finish(step - 3)

    for group in (gz, gx, gc, rc, rx, rz):
        for cp in group.values():
            cp.wait_send()


def body(*args):
    tokens, norm_gain, token_order, gw, gk, ge, uw, uk, ue, dw, dk, de = args
    n = lax.axis_size("tensor")
    Z, X = grid_of(n)
    C = CORES
    R, D = tokens.shape
    F = gw.shape[1]
    T = n * R
    assert TILE % R == 0 and n % TILE == 0 and token_order.shape == (T,)
    G = TILE // R
    KCH, NC = D // QG, D // QR
    half, zr = X * Z * R, Z * R
    fold = max(1, TILE // zr)
    gk, ge, uk, ue = gk.T, ge.T, uk.T, ue.T
    side = D // gk.shape[1]
    V = pltpu.VMEM
    dma = pltpu.SemaphoreType.DMA
    scratch = [
        V((R, D), tokens.dtype), V((1, D), F32), V((1, T), jnp.int32),
        V(gw.shape, BF), V(gk.shape, jnp.int32), V(ge.shape, jnp.int32),
        V(uw.shape, BF), V(uk.shape, jnp.int32), V(ue.shape, jnp.int32),
        V(dw.shape, BF), V(dk.shape, jnp.int32), V(de.shape, jnp.int32),
        V((D // side, F), F32), V((D // side, F), F32), V((F // side, D), F32),
        V((QG, C, X, Z, TILE, KCH // G), BF),
        V((QG, T, KCH), BF),
        V((T, F), F32), V((T, F), F32), V((T, F), BF),
        V((QR, C, half, NC), F32), V((QR, half, NC), BF), V((QR, half, NC), BF),
        V((QR, X, zr, NC), F32),
        V((QR, X - 1, zr * fold, NC // fold), BF), V((QR, X - 1, zr * fold, NC // fold), BF),
        V((QR, Z, TILE, NC // G), BF), V((QR, Z - 1, TILE, NC // G), BF),
        dma((9,)), dma((QG,)), dma((QG,)), dma((QR,)),
        dma((QG, Z - 1)), dma((QG, Z - 1)), dma((QG, X - 1)), dma((QG, X - 1)), dma((QG,)), dma((QG,)),
        dma((QR,)), dma((QR,)), dma((QR, X - 1)), dma((QR, X - 1)), dma((QR, Z - 1)), dma((QR, Z - 1)),
    ]
    out = pl.pallas_call(
        functools.partial(kernel, Z, X),
        out_shape=jax.ShapeDtypeStruct((R, D), F32),
        in_specs=[pl.BlockSpec(memory_space=pl.ANY)] * 12,
        out_specs=pl.BlockSpec(memory_space=pltpu.VMEM),
        scratch_shapes=scratch,
        compiler_params=pltpu.CompilerParams(
            collective_id=0, has_side_effects=True, vmem_limit_bytes=60 * 1024 * 1024
        ),
        cost_estimate=pl.CostEstimate(
            flops=6 * T * D * F, bytes_accessed=6 * D * F, transcendentals=T * F
        ),
    )(tokens, norm_gain.reshape(1, D), token_order.reshape(1, T), gw, gk, ge, uw, uk, ue, dw, dk, de)
    return out.astype(BF)


def solution(mesh):
    return jax.shard_map(
        body,
        mesh=mesh,
        in_specs=(
            P(("groups", "tensor"), None),
            P(),
            P("groups"),
            P(None, "tensor"),
            P(None, "tensor"),
            P(None, "tensor"),
            P(None, "tensor"),
            P(None, "tensor"),
            P(None, "tensor"),
            P("tensor", None),
            P("tensor", None),
            P("tensor", None),
        ),
        out_specs=P(("groups", "tensor"), None),
        check_vma=False,
    )
```

```python
import functools

import jax
import jax.numpy as jnp
from jax import lax
from jax.experimental import pallas as pl
from jax.experimental.pallas import tpu as pltpu
from jax.sharding import PartitionSpec as P

BF = jnp.bfloat16
F32 = jnp.float32
CORES = 2
QG = 2
QR = 2
TILE = 16


def grid_of(n):
    chips = n // CORES
    x = 1
    while (2 * x) * (2 * x) < chips:
        x *= 2
    return chips // x, x


def log2(v):
    return v.bit_length() - 1


def iota(shape, dim):
    return lax.broadcasted_iota(jnp.int32, shape, dim)


def factor(keep, expo):
    power = jnp.where(expo == 0, 1.0, jnp.where(expo > 0, 2.0, 0.5))
    return jnp.where(keep > 0, power, 0.0).astype(F32).astype(BF)


def scale_rows(w, fac, side):
    n = w.shape[0] // side
    cols = w.shape[1]
    parts = []
    for j in range(n):
        row = jnp.broadcast_to(fac[j : j + 1, :], (TILE, cols)).astype(BF)
        block = w[j * side : (j + 1) * side, :].reshape(side // TILE, TILE, cols)
        parts.append((block * row[None]).reshape(side, cols))
    return parts[0] if n == 1 else jnp.concatenate(parts, axis=0)


def kernel(
    Z, X,
    tok_h, gain_h, order_h, gw_h, gk_h, ge_h, uw_h, uk_h, ue_h, dw_h, dk_h, de_h,
    out_ref,
    tok, gain, order, gw, gk, ge, uw, uk, ue, dw, dk, de,
    gfac, ufac, dfac, gbuf, lhs, accg, accu, hid,
    part, csend, crecv, ybuf, xsend, xrecv, zbuf, zrecv,
    small_sem, g_sem, u_sem, d_sem,
    gz_s, gz_r, gx_s, gx_r, gc_s, gc_r,
    rc_s, rc_r, rx_s, rx_r, rz_s, rz_r,
):
    C = CORES
    R, D = tok.shape
    F = gw.shape[1]
    T = C * X * Z * R
    G = TILE // R
    side = D // gk.shape[1]
    KCH = D // QG
    PL = KCH // G
    NC = D // QR
    NCG = NC // G

    me = lax.axis_index("tensor")
    mc = lax.rem(me, C)
    mx = lax.rem(lax.div(me, C), X)
    mz = lax.div(me, C * X)

    def dev(z, x, c):
        return {"tensor": (z * X + x) * C + c}

    def zpeer(d):
        return dev(lax.rem(mz + d, Z), mx, mc)

    def xpeer(d):
        return dev(mz, lax.rem(mx + d, X), mc)

    cpeer = dev(mz, mx, 1 - mc)
    MESH = pl.DeviceIdType.MESH

    barrier = pltpu.get_barrier_semaphore()
    for d in range(1, Z):
        pl.semaphore_signal(barrier, inc=1, device_id=zpeer(d), device_id_type=MESH)
    for d in range(1, X):
        pl.semaphore_signal(barrier, inc=1, device_id=xpeer(d), device_id_type=MESH)
    pl.semaphore_signal(barrier, inc=1, device_id=cpeer, device_id_type=MESH)

    smalls = []
    for i, (a, b) in enumerate(
        ((tok_h, tok), (gain_h, gain), (order_h, order), (gk_h, gk), (ge_h, ge),
         (uk_h, uk), (ue_h, ue), (dk_h, dk), (de_h, de))
    ):
        cp = pltpu.make_async_copy(a, b, small_sem.at[i])
        cp.start()
        smalls.append(cp)
    gcp, ucp, dcp = [], [], []
    for q in range(QG):
        rows = pl.ds(q * KCH, KCH)
        gcp.append(pltpu.make_async_copy(gw_h.at[rows], gw.at[rows], g_sem.at[q]))
        ucp.append(pltpu.make_async_copy(uw_h.at[rows], uw.at[rows], u_sem.at[q]))
        if q == 0:
            gcp[-1].start()
            ucp[-1].start()
    for q in range(QR):
        cols = pl.ds(q * NC, NC)
        dcp.append(pltpu.make_async_copy(dw_h.at[:, cols], dw.at[:, cols], d_sem.at[q]))

    smalls[0].wait()
    smalls[1].wait()
    values = tok[...].astype(F32)
    meansq = jnp.sum(values * values, axis=-1, keepdims=True) * (1.0 / D)
    normed = values * lax.rsqrt(meansq + 1e-05) * gain[...]
    for q in range(QG):
        rowid = iota((TILE, PL), 0)
        piece = jnp.zeros((TILE, PL), F32)
        for g in range(G):
            for i in range(R):
                lo = q * KCH + g * PL
                src = jnp.broadcast_to(normed[i : i + 1, lo : lo + PL], (TILE, PL))
                piece = jnp.where(rowid == g * R + i, src, piece)
        gbuf[q, mc, mx, mz] = piece.astype(BF)

    pl.semaphore_wait(barrier, Z + X - 1)

    def remote(src, dst, s, r, to):
        return pltpu.make_async_remote_copy(
            src_ref=src, dst_ref=dst, send_sem=s, recv_sem=r, device_id=to, device_id_type=MESH
        )

    gz, gx, gc = {}, {}, {}
    for q in range(QG):
        for d in range(1, Z):
            ref = gbuf.at[q, mc, mx, mz]
            gz[q, d] = remote(ref, ref, gz_s.at[q, d - 1], gz_r.at[q, d - 1], zpeer(d))
            gz[q, d].start()

    for s in smalls[2:]:
        s.wait()
    spread = (iota((F // side, F), 1) >> log2(side)) == iota((F // side, F), 0)
    spread = spread.astype(F32).astype(BF)
    outer = (((0,), (0,)), ((), ()))
    gfac[...] = lax.dot_general(factor(gk[...], ge[...]), spread, outer, preferred_element_type=F32)
    ufac[...] = lax.dot_general(factor(uk[...], ue[...]), spread, outer, preferred_element_type=F32)

    def gather_x(q):
        for d in range(1, Z):
            gz[q, d].wait_recv()
        for d in range(1, X):
            ref = gbuf.at[q, mc, mx]
            gx[q, d] = remote(ref, ref, gx_s.at[q, d - 1], gx_r.at[q, d - 1], xpeer(d))
            gx[q, d].start()

    def gather_c(q):
        for d in range(1, X):
            gx[q, d].wait_recv()
        ref = gbuf.at[q, mc]
        gc[q] = remote(ref, ref, gc_s.at[q], gc_r.at[q], cpeer)
        gc[q].start()

    for step in range(QG + 1):
        if step < QG:
            gather_x(step)
            if step + 1 < QG:
                gcp[step + 1].start()
                ucp[step + 1].start()
            else:
                for cp in dcp:
                    cp.start()
        if step >= 1:
            gather_c(step - 1)

    dk_fac = factor(dk[...], de[...])
    for q in range(QR):
        wide = (D // side, NC)
        sel = ((iota(wide, 1) + q * NC) >> log2(side)) == iota(wide, 0)
        dfac[:, q * NC : (q + 1) * NC] = jnp.dot(dk_fac, sel.astype(F32).astype(BF), preferred_element_type=F32)

    def token_of(r):
        i = r & (R - 1)
        z = (r >> log2(R)) & (Z - 1)
        x = (r >> log2(R * Z)) & (X - 1)
        c = r >> log2(R * Z * X)
        return ((z * X + x) * C + c) * R + i

    ones = lambda m: m.astype(F32).astype(BF)
    tt = (T, T)
    s_in = ones(token_of(iota(tt, 0)) == iota(tt, 1))
    s_out = ones(token_of(iota(tt, 1)) == iota(tt, 0))
    mt = ones(iota(tt, 0) == jnp.broadcast_to(order[...], tt))
    pt = jnp.dot(s_in, mt, preferred_element_type=F32).astype(BF)
    pt = jnp.dot(pt, s_out, preferred_element_type=F32)
    pick = pt.T.astype(BF)

    nd = TILE * TILE
    o, s = iota((nd, nd), 0), iota((nd, nd), 1)
    og, od, oi = o >> log2(TILE * R), (o >> log2(R)) & (TILE - 1), o & (R - 1)
    perm = ones(s == od * TILE + og * R + oi)

    KS = 8 * side
    for q in range(QG):
        gc[q].wait_recv()
        rows = gbuf[q].reshape(C * X * Z * TILE, PL)
        for b in range(C * X * Z // TILE):
            y = jnp.dot(perm, rows[b * nd : (b + 1) * nd], preferred_element_type=F32).astype(BF)
            n = TILE * R
            for g in range(G):
                lhs[q, b * n : (b + 1) * n, g * PL : (g + 1) * PL] = y[g * n : (g + 1) * n]
        gcp[q].wait()
        ucp[q].wait()
        if q == 0:
            accg[...] = jnp.zeros_like(accg)
            accu[...] = jnp.zeros_like(accu)

        def gate_up(s, carry, q=q):
            ks = pl.ds(pl.multiple_of(q * KCH + s * KS, KS), KS)
            fs = pl.ds(pl.multiple_of((q * KCH + s * KS) // side, 8), 8)
            left = lhs[q, :, pl.ds(pl.multiple_of(s * KS, KS), KS)]
            wg = scale_rows(gw[ks, :], gfac[fs, :], side)
            accg[...] += jnp.dot(left, wg, preferred_element_type=F32)
            wu = scale_rows(uw[ks, :], ufac[fs, :], side)
            accu[...] += jnp.dot(left, wu, preferred_element_type=F32)
            return carry

        lax.fori_loop(0, KCH // KS, gate_up, 0, unroll=4)

    gate = accg[...]
    hidden = (gate / (1.0 + jnp.exp(-gate)) * accu[...]).astype(BF)
    hid[...] = jnp.dot(pick, hidden, preferred_element_type=F32).astype(BF)

    half = X * Z * R
    fold = max(1, TILE // (Z * R))
    zr = Z * R
    zn = G * zr
    o, s = iota((zn, zn), 0), iota((zn, zn), 1)
    oz, og, oi = o >> log2(TILE), (o >> log2(R)) & (G - 1), o & (R - 1)
    perm_z = ones(s == og * zr + oz * R + oi)

    rc, rx, rz = {}, {}, {}

    def folded(v):
        w = NC // fold
        return jnp.concatenate([v[:, h * w : (h + 1) * w] for h in range(fold)], axis=0) if fold > 1 else v

    NS = 512

    def down(q):
        dcp[q].wait()

        def tile(n, carry):
            cols = pl.ds(pl.multiple_of(q * NC + n * NS, NS), NS)
            w = scale_rows(dw[:, cols], dfac[:, cols], side)
            y = jnp.dot(hid[...], w, preferred_element_type=F32)
            part[q, :, :, pl.ds(pl.multiple_of(n * NS, NS), NS)] = y.reshape(C, half, NS)
            return carry

        lax.fori_loop(0, NC // NS, tile, 0, unroll=4)
        csend[q] = part[q, 1 - mc].astype(BF)
        rc[q] = remote(csend.at[q], crecv.at[q], rc_s.at[q], rc_r.at[q], cpeer)
        rc[q].start()

    def reduce_x(q):
        rc[q].wait_recv()
        ybuf[q] = (part[q, mc] + crecv[q].astype(F32)).reshape(X, zr, NC)
        for d in range(1, X):
            xsend[q, d - 1] = folded(ybuf[q, lax.rem(mx + d, X)]).astype(BF)
            rx[q, d] = remote(
                xsend.at[q, d - 1], xrecv.at[q, d - 1], rx_s.at[q, d - 1], rx_r.at[q, d - 1], xpeer(d)
            )
            rx[q, d].start()

    def reduce_z(q):
        y = folded(ybuf[q, mx])
        for d in range(1, X):
            rx[q, d].wait_recv()
            y = y + xrecv[q, d - 1].astype(F32)
        per = G // fold
        stack = [
            y[(g // per) * zr : (g // per + 1) * zr, (g % per) * NCG : (g % per + 1) * NCG] for g in range(G)
        ]
        stack = jnp.concatenate(stack, axis=0).astype(BF)
        zbuf[q] = jnp.dot(perm_z, stack, preferred_element_type=F32).astype(BF).reshape(Z, TILE, NCG)
        for d in range(1, Z):
            rz[q, d] = remote(
                zbuf.at[q, lax.rem(mz + d, Z)], zrecv.at[q, d - 1],
                rz_s.at[q, d - 1], rz_r.at[q, d - 1], zpeer(d),
            )
            rz[q, d].start()

    def finish(q):
        y = zbuf[q, mz].astype(F32)
        for d in range(1, Z):
            rz[q, d].wait_recv()
            y = y + zrecv[q, d - 1].astype(F32)
        for g in range(G):
            for i in range(R):
                lo = q * NC + g * NCG
                out_ref[i : i + 1, lo : lo + NCG] = y[g * R + i : g * R + i + 1]

    for step in range(QR + 3):
        if step < QR:
            down(step)
        if 0 <= step - 1 < QR:
            reduce_x(step - 1)
        if 0 <= step - 2 < QR:
            reduce_z(step - 2)
        if 0 <= step - 3 < QR:
            finish(step - 3)

    for group in (gz, gx, gc, rc, rx, rz):
        for cp in group.values():
            cp.wait_send()


def body(*args):
    tokens, norm_gain, token_order, gw, gk, ge, uw, uk, ue, dw, dk, de = args
    n = lax.axis_size("tensor")
    Z, X = grid_of(n)
    C = CORES
    R, D = tokens.shape
    F = gw.shape[1]
    T = n * R
    assert TILE % R == 0 and n % TILE == 0 and token_order.shape == (T,)
    G = TILE // R
    KCH, NC = D // QG, D // QR
    half, zr = X * Z * R, Z * R
    fold = max(1, TILE // zr)
    gk, ge, uk, ue = gk.T, ge.T, uk.T, ue.T
    side = D // gk.shape[1]
    V = pltpu.VMEM
    dma = pltpu.SemaphoreType.DMA
    scratch = [
        V((R, D), tokens.dtype), V((1, D), F32), V((1, T), jnp.int32),
        V(gw.shape, BF), V(gk.shape, jnp.int32), V(ge.shape, jnp.int32),
        V(uw.shape, BF), V(uk.shape, jnp.int32), V(ue.shape, jnp.int32),
        V(dw.shape, BF), V(dk.shape, jnp.int32), V(de.shape, jnp.int32),
        V((D // side, F), F32), V((D // side, F), F32), V((F // side, D), F32),
        V((QG, C, X, Z, TILE, KCH // G), BF),
        V((QG, T, KCH), BF),
        V((T, F), F32), V((T, F), F32), V((T, F), BF),
        V((QR, C, half, NC), F32), V((QR, half, NC), BF), V((QR, half, NC), BF),
        V((QR, X, zr, NC), F32),
        V((QR, X - 1, zr * fold, NC // fold), BF), V((QR, X - 1, zr * fold, NC // fold), BF),
        V((QR, Z, TILE, NC // G), BF), V((QR, Z - 1, TILE, NC // G), BF),
        dma((9,)), dma((QG,)), dma((QG,)), dma((QR,)),
        dma((QG, Z - 1)), dma((QG, Z - 1)), dma((QG, X - 1)), dma((QG, X - 1)), dma((QG,)), dma((QG,)),
        dma((QR,)), dma((QR,)), dma((QR, X - 1)), dma((QR, X - 1)), dma((QR, Z - 1)), dma((QR, Z - 1)),
    ]
    out = pl.pallas_call(
        functools.partial(kernel, Z, X),
        out_shape=jax.ShapeDtypeStruct((R, D), F32),
        in_specs=[pl.BlockSpec(memory_space=pl.ANY)] * 12,
        out_specs=pl.BlockSpec(memory_space=pltpu.VMEM),
        scratch_shapes=scratch,
        compiler_params=pltpu.CompilerParams(
            collective_id=0, has_side_effects=True, vmem_limit_bytes=60 * 1024 * 1024
        ),
        cost_estimate=pl.CostEstimate(
            flops=6 * T * D * F, bytes_accessed=6 * D * F, transcendentals=T * F
        ),
    )(tokens, norm_gain.reshape(1, D), token_order.reshape(1, T), gw, gk, ge, uw, uk, ue, dw, dk, de)
    return out.astype(BF)


def solution(mesh):
    return jax.shard_map(
        body,
        mesh=mesh,
        in_specs=(
            P(("groups", "tensor"), None),
            P(),
            P("groups"),
            P(None, "tensor"),
            P(None, "tensor"),
            P(None, "tensor"),
            P(None, "tensor"),
            P(None, "tensor"),
            P(None, "tensor"),
            P("tensor", None),
            P("tensor", None),
            P("tensor", None),
        ),
        out_specs=P(("groups", "tensor"), None),
        check_vma=False,
    )
```
